512 devices in a mesh: user: 32 (over x_lo, z), feat: 8 (over y, x_hi), dom: 2 (over core).
Axes of the slice: x: 4 (x_hi: 2, x_lo: 2; x = x_hi * 2 + x_lo), y: 4, z: 16, core: 2. Of those that a mesh axis runs over, the one named last changes fastest.
Arguments:
- side_matrix: bfloat16 [16384, 16384], P('user', ('feat', 'dom')), may hold values from -6 to 6
- slab: bfloat16 [8, 256, 16384], P('dom', 'feat', 'user'), may hold values from -6 to 6
- user_factor: bfloat16 [16384, 512], P('user'), may hold values from -6 to 6
- feat_factor: bfloat16 [512, 16384], P('user', ('feat', 'dom')), may hold values from -0.25 to 0.25
- item_factor: bfloat16 [256, 512], P('feat'), may hold values from -6 to 6
- domain_factor: bfloat16 [8, 512], P('dom'), may hold values from -0.25 to 0.25
Outputs:
- grad_user: float32 [16384, 512], P('user', ('feat', 'dom'))
- grad_feat: float32 [512, 16384], P('user', ('feat', 'dom'))
- grad_item: float32 [256, 512], P('feat')
- grad_domain: float32 [8, 512], P('dom')
The draws below stay inside these ranges and needn't reach their ends.
All inputs are finite; a program needn't handle non-finite values.
Results may differ from the reference program's by a relative error of at most 0.0017.
Values may be sent and summed in bfloat16 or wider, within the bound.
A program may use at most 64 MiB of HBM per device.

```python
import math
import jax
import jax.numpy as jnp
from jax import lax

RANK = 512
FEATS = 16384
ITEMS = 256
DOMS = 8
USER_DEV = 512
USERS = 16384


def levels(stream_key, shape, split, smallest, top_value):
    loudness = 1.0
    for axis_at, shards_of in split:
        heights = jax.random.uniform(jax.random.fold_in(jax.random.fold_in(stream_key, 6), axis_at), (shards_of,), jnp.float32, smallest / len(split), top_value / len(split))
        loudness = loudness * jnp.repeat(jnp.exp(heights), shape[axis_at] // shards_of).reshape((-1,) + (1,) * (len(shape) - 1 - axis_at))
    return loudness


def centred(own_key, dims, spread, most, shards=(), dtype=jnp.bfloat16):
    entries = jax.random.normal(own_key, dims, jnp.float32) * spread
    if len(shards) > 0:
        entries = levels(own_key, dims, shards, -0.22, 0.18) * entries
    return jnp.clip(entries, min=-most, max=most).astype(dtype)


def setup_inputs(seed: int = 0) -> dict:
    arg_keys = jax.random.split(jax.random.key(seed), 7)
    return {
        "side_matrix": centred(arg_keys[0], (USERS, FEATS), 1.0, 6.0, ((0, 32), (1, 16))),
        "slab": centred(arg_keys[1], (DOMS, ITEMS, USERS), 1.0, 6.0, ((0, 2), (1, 8), (2, 32))),
        "user_factor": centred(arg_keys[2], (USERS, RANK), 1.0, 6.0, ((0, 32),)),
        "feat_factor": centred(arg_keys[3], (RANK, FEATS), RANK ** -0.5, 0.25, ((0, 32), (1, 16))),
        "item_factor": centred(arg_keys[4], (ITEMS, RANK), 1.0, 6.0, ((0, 8),)),
        "domain_factor": centred(arg_keys[5], (DOMS, RANK), RANK ** -0.5, 0.25, ((0, 2),)),
    }


def reference(side_matrix, slab, user_factor, feat_factor, item_factor, domain_factor):
    domain_item = (domain_factor.astype(jnp.float32)[:, None, :] * item_factor.astype(jnp.float32)[None, :, :]).astype(jnp.bfloat16).reshape(DOMS * ITEMS, RANK)
    tensor_model = jnp.dot(domain_item, user_factor.T, preferred_element_type=jnp.float32)
    tensor_res = (tensor_model - slab.reshape(DOMS * ITEMS, USERS).astype(jnp.float32)).astype(jnp.bfloat16)
    tensor_user = jnp.dot(tensor_res.T, domain_item, preferred_element_type=jnp.float32) * math.sqrt(RANK / (ITEMS * DOMS))
    projected = jnp.dot(tensor_res, user_factor, preferred_element_type=jnp.float32).reshape(DOMS, ITEMS, RANK)
    grad_item = math.sqrt(RANK / (USERS * DOMS)) * lax.optimization_barrier(jnp.sum(projected * domain_factor.astype(jnp.float32)[:, None, :], axis=0))
    grad_domain = lax.optimization_barrier(jnp.sum(projected * item_factor.astype(jnp.float32)[None, :, :], axis=1)) / math.sqrt(USERS * ITEMS)
    blocks = USERS // USER_DEV
    side_blocks = side_matrix.reshape(blocks, USER_DEV, FEATS)
    user_blocks = user_factor.reshape(blocks, USER_DEV, RANK)
    tensor_blocks = tensor_user.reshape(blocks, USER_DEV, RANK)
    side_scale = math.sqrt(RANK / FEATS)
    feat_scale = 1.0 / math.sqrt(USERS)

    def accumulate(carry, inputs):
        side_block, user_block, tensor_block = inputs
        side_model = jnp.dot(user_block, feat_factor, preferred_element_type=jnp.float32)
        side_res = (side_model - side_block.astype(jnp.float32)).astype(jnp.bfloat16)
        user_grad = side_scale * jnp.dot(side_res, feat_factor.T, preferred_element_type=jnp.float32) + tensor_block
        partial_grad = jnp.dot(user_block.T, side_res, preferred_element_type=jnp.float32) * feat_scale
        return (carry + partial_grad, user_grad)
    grad_feat, user_grads = lax.scan(accumulate, jnp.zeros((RANK, FEATS), jnp.float32), (side_blocks, user_blocks, tensor_blocks))
    grad_user = user_grads.reshape(USERS, RANK)
    return (grad_user, grad_feat, grad_item, grad_domain)
```

```python
import math

import jax
import jax.numpy as jnp
from jax import lax
from jax.experimental import pallas as pl
from jax.experimental.pallas import tpu as pltpu
from jax.sharding import PartitionSpec as P

MESH = pl.DeviceIdType.MESH
F32, BF16 = jnp.float32, jnp.bfloat16

RANK = 512
FEATS = 16384
ITEMS = 256
DOMS = 8
USERS = 16384

NZ = 16
ROWS = 16
CHUNKS = 2
HUBS = (0, 3, -3, 6, -6)
SLOTS = HUBS + tuple(h - 1 for h in HUBS) + tuple(h + 1 for h in HUBS) + (8,)

SIDE_SCALE = math.sqrt(RANK / FEATS)
TENSOR_SCALE = math.sqrt(RANK / (ITEMS * DOMS))
FEAT_SCALE = 1.0 / math.sqrt(USERS)
ITEM_SCALE = math.sqrt(RANK / (USERS * DOMS))
DOMAIN_SCALE = 1.0 / math.sqrt(USERS * ITEMS)

N_MESSAGES = 96
N_LOCAL = 8


def dot(a, b, ca=1, cb=0):
    return lax.dot_general(a, b, (((ca,), (cb,)), ((), ())), preferred_element_type=F32)


def kernel(
    side_h, slab_h, user_h, feat_h, item_h, domain_h,
    gu_ref, gf_ref, gi_ref, gd_ref,
    side, slab, user, items, domains,
    panel, user_rel, ut_abs, ut_rel,
    model_di, tensor_res, small, small_abs, tensor_user, side_user,
    gf_other, gf_own, gf_x, gf_send, gf_near, gf_far8, gf_hub, gf_far,
    sx_other, sx_own, sx_x, sx_send, sx_near, sx_far8, sx_hub, sx_far,
    row_send, row_recv, small_panel,
    su_all, su_core, su_core_recv, su_sum, su_send, su_recv,
    send_sems, recv_sems, local_sems,
):
    u, f, d = lax.axis_index("user"), lax.axis_index("feat"), lax.axis_index("dom")
    xl, z = u // NZ, u % NZ
    width = panel.shape[-1]

    def along(dz=0, dx=0):
        return ((xl + dx) % 2 * NZ + (z + dz + NZ) % NZ, f, d)

    def across(df):
        return (u, (f + df) % 8, d)

    partner = (u, f, 1 - d)
    counter = [0]

    def send(src, dst, device):
        i = counter[0]
        counter[0] += 1
        copy = pltpu.make_async_remote_copy(
            src, dst, send_sems.at[i], recv_sems.at[i], device_id=device, device_id_type=MESH
        )
        copy.start()
        sent.append(copy)
        return copy

    sent = []

    feat_copies = [
        pltpu.make_async_copy(
            feat_h.at[:, pl.ds(c * width, width)], panel.at[c, 0, 0], local_sems.at[c]
        )
        for c in range(CHUNKS)
    ]
    user_copy = pltpu.make_async_copy(user_h, user, local_sems.at[CHUNKS])
    item_copy = pltpu.make_async_copy(item_h, items, local_sems.at[CHUNKS + 1])
    domain_copy = pltpu.make_async_copy(domain_h, domains, local_sems.at[CHUNKS + 2])
    slab_copy = pltpu.make_async_copy(slab_h, slab, local_sems.at[CHUNKS + 3])
    side_copy = pltpu.make_async_copy(side_h, side, local_sems.at[CHUNKS + 4])
    for copy in feat_copies + [user_copy, item_copy, domain_copy, slab_copy, side_copy]:
        copy.start()

    barrier = pltpu.get_barrier_semaphore()
    greet = [along(dz) for dz in (1, -1, 2, -2, 3, -3, 6, -6)] + [along(0, 1), partner]
    greet += [across(df) for df in range(1, 8)]
    for device in greet:
        pl.semaphore_signal(barrier, inc=1, device_id=device, device_id_type=MESH)
    pl.semaphore_wait(barrier, len(greet))

    def gather_start(g):
        far = [send(g.at[0, 0], g.at[0, h], along(-HUBS[h])) for h in range(1, 5)]
        near = [send(g.at[0, 0], g.at[0, 5], along(1)), send(g.at[0, 0], g.at[0, 10], along(-1))]
        other = [send(g.at[0, 0], g.at[1, 0], along(0, 1))]
        return far, near, other

    def gather_near(g, state):
        far, near, other = state
        for lo in (1, 3):
            for copy in far[lo - 1 : lo + 1]:
                copy.wait_recv()
            two = pl.ds(lo, 2)
            near.append(send(g.at[0, two], g.at[0, pl.ds(5 + lo, 2)], along(1)))
            near.append(send(g.at[0, two], g.at[0, pl.ds(10 + lo, 2)], along(-1)))
        near.append(send(g.at[0, 3], g.at[0, 15], along(-2)))
        other.append(send(g.at[0, pl.ds(1, 4)], g.at[1, pl.ds(1, 4)], along(0, 1)))

    def gather_other(g, state):
        far, near, other = state
        for copy in near:
            copy.wait_recv()
        other.append(send(g.at[0, pl.ds(5, 11)], g.at[1, pl.ds(5, 11)], along(0, 1)))

    def gather_end(state):
        for copy in state[2]:
            copy.wait_recv()

    def reduce_near(own, x, stage, near, far8, state):
        for copy in state:
            copy.wait_recv()
        stage[...] = (own[5:] + x[5:].astype(F32)).astype(BF16)
        copies = [
            send(stage.at[pl.ds(5, 5)], near.at[0], along(1)),
            send(stage.at[pl.ds(0, 5)], near.at[1], along(-1)),
            send(stage.at[10], far8, along(2)),
        ]
        own[:5] = own[:5] + x[:5].astype(F32)
        return copies

    def reduce_far(own, near, far8, hub, far, state):
        for copy in state:
            copy.wait_recv()
        own[:5] = own[:5] + near[0].astype(F32) + near[1].astype(F32)
        own[3] = own[3] + far8[...].astype(F32)
        hub[...] = own[1:5].astype(BF16)
        return [send(hub.at[h - 1], far.at[h - 1], along(HUBS[h])) for h in range(1, 5)]

    def reduce_end(own, far, state):
        for copy in state:
            copy.wait_recv()
        total = own[0]
        for h in range(4):
            total = total + far[h].astype(F32)
        return total

    gathers = []
    for c in range(CHUNKS):
        feat_copies[c].wait()
        gathers.append(gather_start(panel.at[c]))

    def absolute(plane, slot):
        return (xl + plane) % 2 * NZ + (z + SLOTS[slot] + NZ) % NZ

    user_copy.wait()
    item_copy.wait()
    domain_copy.wait()
    slab_copy.wait()
    for k in range(4):
        model_di[32 * k : 32 * k + 32, :] = (
            domains[k : k + 1, :].astype(F32) * items[...].astype(F32)
        ).astype(BF16)
    tensor_res[...] = (
        dot(model_di[...], user[...], 1, 1) - slab[...].reshape(128, 512).astype(F32)
    ).astype(BF16)
    projected = dot(tensor_res[...], user[...])
    item_term = jnp.zeros((32, RANK), F32)
    small[...] = jnp.zeros_like(small)
    for k in range(4):
        part = projected[32 * k : 32 * k + 32, :]
        item_term = item_term + part * domains[k : k + 1, :].astype(F32)
        small[32 + k : 33 + k, :] = DOMAIN_SCALE * jnp.sum(
            part * items[...].astype(F32), axis=0, keepdims=True
        )
    small[0:32, :] = ITEM_SCALE * item_term
    small_abs[...] = small[...].T.reshape(32, ROWS, 128)
    for slot in range(NZ):
        sx_other[slot] = small_abs[absolute(1, slot)].astype(BF16)
        sx_own[slot] = small_abs[absolute(0, slot)]
    sx_state = [send(sx_other, sx_x, along(0, 1))]

    ut_abs[...] = user[...].T.reshape(32, ROWS, 512)
    for plane in range(2):
        for slot in range(NZ):
            ut_rel[plane, slot] = ut_abs[absolute(plane, slot)]
    user_rel[...] = ut_rel[...].reshape(512, 512).T

    gather_near(panel.at[0], gathers[0])
    tensor_user[...] = (
        TENSOR_SCALE * dot(model_di[...], tensor_res[...], 0, 0)
    ).reshape(32, ROWS, 512)
    gather_near(panel.at[1], gathers[1])
    sx_state = reduce_near(sx_own, sx_x, sx_send, sx_near, sx_far8, sx_state)
    gather_other(panel.at[0], gathers[0])
    gather_other(panel.at[1], gathers[1])
    sx_state = reduce_far(sx_own, sx_near, sx_far8, sx_hub, sx_far, sx_state)

    side_copy.wait()
    gf_state = []

    def compute(c):
        gather_end(gathers[c])
        block = panel[c].reshape(512, width)
        res = (
            dot(user_rel[...], block) - side[:, c * width : (c + 1) * width].astype(F32)
        ).astype(BF16)
        gf_other[c] = dot(ut_rel[1].reshape(256, 512), res).reshape(NZ, ROWS, width).astype(BF16)
        gf_state.append([send(gf_other.at[c], gf_x.at[c], along(0, 1))])
        gf_own[c] = dot(ut_rel[0].reshape(256, 512), res).reshape(NZ, ROWS, width)
        part = dot(block, res, 1, 1).reshape(32, ROWS, 512)
        if c == 0:
            side_user[...] = part
        else:
            side_user[...] = side_user[...] + part

    compute(0)

    total = reduce_end(sx_own, sx_far, sx_state)
    row_send[...] = total
    row_copies = [send(row_send, row_recv.at[0], partner)]
    row_copies += [send(row_send, row_recv.at[df], across(df)) for df in range(1, 8)]

    compute(1)

    for plane in range(2):
        for slot in range(NZ):
            b = absolute(plane, slot)
            place = (b // 2 + d) % 2 * 16 + b // 4 * 2 + b % 2
            su_all[place] = SIDE_SCALE * side_user[plane * NZ + slot] + tensor_user[b]
    su_core[...] = su_all[16:].astype(BF16)
    su_copy = send(su_core, su_core_recv, partner)

    def gf_near_step(c):
        gf_state[c] = reduce_near(
            gf_own.at[c], gf_x.at[c], gf_send.at[c], gf_near.at[c], gf_far8.at[c], gf_state[c]
        )

    def gf_far_step(c):
        gf_state[c] = reduce_far(
            gf_own.at[c], gf_near.at[c], gf_far8.at[c], gf_hub.at[c], gf_far.at[c], gf_state[c]
        )

    gf_near_step(0)
    for copy in row_copies:
        copy.wait_recv()
    lane = lax.broadcasted_iota(jnp.int32, (ROWS, 128), 1)
    feats = row_recv[1]
    for df in range(2, 8):
        feats = feats + row_recv[df]
    small_panel[0, 0] = total + jnp.where(lane < 32, row_recv[0], feats)
    small_gather = gather_start(small_panel)

    gf_near_step(1)
    su_copy.wait_recv()
    su_sum[...] = (su_all[:16] + su_core_recv[...].astype(F32)).reshape(8, 32, 512)
    su_send[...] = su_sum[...].astype(BF16)
    su_copies = [
        send(su_send.at[(f + df) % 8], su_recv.at[df - 1], across(df)) for df in range(1, 8)
    ]
    gf_far_step(0)
    gather_near(small_panel, small_gather)
    gf_far_step(1)
    gather_other(small_panel, small_gather)

    gf_ref[:, 0:width] = FEAT_SCALE * reduce_end(gf_own.at[0], gf_far.at[0], gf_state[0])
    for copy in su_copies:
        copy.wait_recv()
    grad = su_sum[f]
    for df in range(7):
        grad = grad + su_recv[df].astype(F32)
    gu_ref[...] = grad
    gather_end(small_gather)
    for plane in range(2):
        for slot in range(NZ):
            small_abs[absolute(plane, slot)] = small_panel[plane, slot]
    small[...] = small_abs[...].reshape(512, 128).T
    gi_ref[...] = small[0:32, :]
    gd_ref[...] = small[32:36, :]
    gf_ref[:, width:] = FEAT_SCALE * reduce_end(gf_own.at[1], gf_far.at[1], gf_state[1])
    for copy in sent:
        copy.wait_send()


def local(side_matrix, slab, user_factor, feat_factor, item_factor, domain_factor):
    width = 1024 // CHUNKS

    def reduction(lead, w):
        return [
            pltpu.VMEM(lead + (NZ, ROWS, w), BF16),
            pltpu.VMEM(lead + (NZ, ROWS, w), F32),
            pltpu.VMEM(lead + (NZ, ROWS, w), BF16),
            pltpu.VMEM(lead + (11, ROWS, w), BF16),
            pltpu.VMEM(lead + (2, 5, ROWS, w), BF16),
            pltpu.VMEM(lead + (ROWS, w), BF16),
            pltpu.VMEM(lead + (4, ROWS, w), BF16),
            pltpu.VMEM(lead + (4, ROWS, w), BF16),
        ]

    grad_user, grad_feat, grad_item, grad_domain = pl.pallas_call(
        kernel,
        out_shape=(
            jax.ShapeDtypeStruct((32, 512), F32),
            jax.ShapeDtypeStruct((ROWS, 1024), F32),
            jax.ShapeDtypeStruct((32, RANK), F32),
            jax.ShapeDtypeStruct((4, RANK), F32),
        ),
        in_specs=[pl.BlockSpec(memory_space=pl.ANY)] * 6,
        out_specs=[pl.BlockSpec(memory_space=pltpu.VMEM)] * 4,
        scratch_shapes=[
            pltpu.VMEM((512, 1024), BF16),
            pltpu.VMEM((4, 32, 512), BF16),
            pltpu.VMEM((512, 512), BF16),
            pltpu.VMEM((32, 512), BF16),
            pltpu.VMEM((4, 512), BF16),
            pltpu.VMEM((CHUNKS, 2, NZ, ROWS, width), BF16),
            pltpu.VMEM((512, 512), BF16),
            pltpu.VMEM((32, ROWS, 512), BF16),
            pltpu.VMEM((2, NZ, ROWS, 512), BF16),
            pltpu.VMEM((128, 512), BF16),
            pltpu.VMEM((128, 512), BF16),
            pltpu.VMEM((128, 512), F32),
            pltpu.VMEM((32, ROWS, 128), F32),
            pltpu.VMEM((32, ROWS, 512), F32),
            pltpu.VMEM((32, ROWS, 512), F32),
        ]
        + reduction((CHUNKS,), width)
        + reduction((), 128)
        + [
            pltpu.VMEM((ROWS, 128), F32),
            pltpu.VMEM((8, ROWS, 128), F32),
            pltpu.VMEM((2, NZ, ROWS, 128), F32),
            pltpu.VMEM((32, ROWS, 512), F32),
            pltpu.VMEM((16, ROWS, 512), BF16),
            pltpu.VMEM((16, ROWS, 512), BF16),
            pltpu.VMEM((8, 32, 512), F32),
            pltpu.VMEM((8, 32, 512), BF16),
            pltpu.VMEM((7, 32, 512), BF16),
            pltpu.SemaphoreType.DMA((N_MESSAGES,)),
            pltpu.SemaphoreType.DMA((N_MESSAGES,)),
            pltpu.SemaphoreType.DMA((N_LOCAL,)),
        ],
        compiler_params=pltpu.CompilerParams(
            collective_id=0, has_side_effects=True, vmem_limit_bytes=48 << 20
        ),
        name="factor_gradients",
    )(side_matrix, slab, user_factor, feat_factor, item_factor, domain_factor)
    return grad_user.T, grad_feat, grad_item, grad_domain


def solution(mesh):
    return jax.shard_map(
        local,
        mesh=mesh,
        in_specs=(
            P("user", ("feat", "dom")),
            P("dom", "feat", "user"),
            P("user", None),
            P("user", ("feat", "dom")),
            P("feat", None),
            P("dom", None),
        ),
        out_specs=(
            P("user", ("feat", "dom")),
            P("user", ("feat", "dom")),
            P("feat", None),
            P("dom", None),
        ),
        check_vma=False,
    )
```

```python
import math

import jax
import jax.numpy as jnp
from jax import lax
from jax.experimental import pallas as pl
from jax.experimental.pallas import tpu as pltpu
from jax.sharding import PartitionSpec as P

MESH = pl.DeviceIdType.MESH
F32, BF16 = jnp.float32, jnp.bfloat16

RANK = 512
FEATS = 16384
ITEMS = 256
DOMS = 8
USERS = 16384

NZ = 16
ROWS = 16
CHUNKS = 2
HUBS = (0, 3, -3, 6, -6)
SLOTS = tuple(h + j for h in HUBS for j in (0, -1, 1)) + (8,)

SIDE_SCALE = math.sqrt(RANK / FEATS)
TENSOR_SCALE = math.sqrt(RANK / (ITEMS * DOMS))
FEAT_SCALE = 1.0 / math.sqrt(USERS)
ITEM_SCALE = math.sqrt(RANK / (USERS * DOMS))
DOMAIN_SCALE = 1.0 / math.sqrt(USERS * ITEMS)

N_MESSAGES = 128
N_LOCAL = 8


def dot(a, b, ca=1, cb=0):
    return lax.dot_general(a, b, (((ca,), (cb,)), ((), ())), preferred_element_type=F32)


def kernel(
    side_h, slab_h, user_h, feat_h, item_h, domain_h,
    gu_ref, gf_ref, gi_ref, gd_ref,
    side, slab, user, items, domains,
    panel, user_rel, ut_abs, ut_rel,
    model_di, tensor_res, small, small_abs, tensor_user, side_user,
    gf_other, gf_own, gf_x, gf_send, gf_near, gf_hub, gf_far,
    sx_other, sx_own, sx_x, sx_send, sx_near, sx_hub, sx_far,
    row_send, row_recv, row_y, small_panel,
    su_all, su_core, su_core_recv, su_sum, su_send, su_recv, su_y, su_x,
    send_sems, recv_sems, local_sems,
):
    u, f, d = lax.axis_index("user"), lax.axis_index("feat"), lax.axis_index("dom")
    xl, z, y, xh = u // NZ, u % NZ, f // 2, f % 2
    width = panel.shape[-1]

    def along(dz=0, dx=0):
        return ((xl + dx) % 2 * NZ + (z + dz + NZ) % NZ, f, d)

    def beside(dy):
        return (u, (y + dy) % 4 * 2 + xh, d)

    partner, opposite = (u, f, 1 - d), (u, y * 2 + 1 - xh, d)
    counter = [0]

    def send(src, dst, device):
        i = counter[0]
        counter[0] += 1
        copy = pltpu.make_async_remote_copy(
            src, dst, send_sems.at[i], recv_sems.at[i], device_id=device, device_id_type=MESH
        )
        copy.start()
        sent.append(copy)
        return copy

    sent = []

    feat_copies = [
        pltpu.make_async_copy(
            feat_h.at[:, pl.ds(c * width, width)], panel.at[c, 0, 0, 0], local_sems.at[c]
        )
        for c in range(CHUNKS)
    ]
    user_copy = pltpu.make_async_copy(user_h, user, local_sems.at[CHUNKS])
    item_copy = pltpu.make_async_copy(item_h, items, local_sems.at[CHUNKS + 1])
    domain_copy = pltpu.make_async_copy(domain_h, domains, local_sems.at[CHUNKS + 2])
    slab_copy = pltpu.make_async_copy(slab_h, slab, local_sems.at[CHUNKS + 3])
    side_copy = pltpu.make_async_copy(side_h, side, local_sems.at[CHUNKS + 4])
    for copy in feat_copies + [user_copy, item_copy, domain_copy, slab_copy, side_copy]:
        copy.start()

    barrier = pltpu.get_barrier_semaphore()
    greet = [along(dz) for dz in (1, -1, 2, -2, 3, -3)] + [along(0, 1), partner]
    greet += [beside(dy) for dy in range(1, 4)] + [opposite]
    for device in greet:
        pl.semaphore_signal(barrier, inc=1, device_id=device, device_id_type=MESH)
    pl.semaphore_wait(barrier, len(greet))

    def gather_start(g):
        own = g.at[0, 0, 0]
        far = [send(own, g.at[0, h, 0], along(-HUBS[h])) for h in (1, 2)]
        near = [send(own, g.at[0, 0, 1], along(1)), send(own, g.at[0, 0, 2], along(-1))]
        return {"far": far, "near": near, "other": []}

    def gather_own(g, state):
        for copy in state["near"]:
            copy.wait_recv()
        state["other"].append(send(g.at[0, 0], g.at[1, 0], along(0, 1)))

    def gather_hubs(g, state, lo):
        for copy in state["far"]:
            copy.wait_recv()
        if lo == 1:
            state["far"] = [
                send(g.at[0, h, 0], g.at[0, h + 2, 0], along(-HUBS[h])) for h in (1, 2)
            ]
        two = pl.ds(lo, 2)
        hub = g.at[0, two, 0]
        state["near"] = [send(hub, g.at[0, two, 1], along(1)), send(hub, g.at[0, two, 2], along(-1))]
        if lo == 3:
            state["near"].append(send(g.at[0, 3, 0], g.at[0, 5, 0], along(-2)))
            state["other"].append(send(hub, g.at[1, two, 0], along(0, 1)))

    def gather_near(g, state, lo):
        for copy in state["near"]:
            copy.wait_recv()
        two = pl.ds(lo, 2)
        if lo == 3:
            rest = pl.ds(1, 2)
            state["other"].append(send(g.at[0, two, rest], g.at[1, two, rest], along(0, 1)))
            state["other"].append(send(g.at[0, 5, 0], g.at[1, 5, 0], along(0, 1)))
        else:
            state["other"].append(send(g.at[0, two], g.at[1, two], along(0, 1)))

    def gather_end(state):
        for copy in state["other"]:
            copy.wait_recv()

    groups = ((9, 16), (3, 9), (0, 3))

    def reduce_start(other, x):
        parts = [pl.ds(lo, hi - lo) for lo, hi in groups]
        return {"x": [send(other.at[p], x.at[p], along(0, 1)) for p in parts], "near": {}, "far": []}

    def reduce_near(own, x, stage, near, state, i):
        lo, hi = groups[i]
        state["x"][i].wait_recv()
        total = own[lo:hi] + x[lo:hi].astype(F32)
        own[lo:hi] = total
        first, count = lo // 3, (hi - lo) // 3
        for h in range(count):
            stage[first + h] = total[3 * h : 3 * h + 3].astype(BF16)
        some = pl.ds(first, count)
        state["near"][i] = [
            send(stage.at[some, 2], near.at[some, 2], along(1)),
            send(stage.at[some, 1], near.at[some, 1], along(-1)),
        ]
        if i == 0:
            stage[5, 0] = total[6].astype(BF16)
            state["near"][i].append(send(stage.at[5, 0], near.at[5, 0], along(2)))

    def reduce_far(own, near, hub, far, state, i):
        for copy in state["near"][i]:
            copy.wait_recv()
        lo, hi = groups[i]
        for h in range(lo // 3, lo // 3 + (hi - lo) // 3):
            total = own[3 * h] + near[h, 1].astype(F32) + near[h, 2].astype(F32)
            if h == 3:
                total = total + near[5, 0].astype(F32)
            if h == 0:
                own[0] = total
            else:
                hub[h - 1] = total.astype(BF16)
                state["far"].append(send(hub.at[h - 1], far.at[h - 1], along(HUBS[h])))

    def reduce_end(own, far, state):
        for copy in state["far"]:
            copy.wait_recv()
        total = own[0]
        for h in range(4):
            total = total + far[h].astype(F32)
        return total

    gathers = []
    for c in range(CHUNKS):
        feat_copies[c].wait()
        gathers.append(gather_start(panel.at[c]))

    def absolute(plane, slot):
        return (xl + plane) % 2 * NZ + (z + SLOTS[slot] + NZ) % NZ

    user_copy.wait()
    item_copy.wait()
    domain_copy.wait()
    slab_copy.wait()
    for k in range(4):
        model_di[32 * k : 32 * k + 32, :] = (
            domains[k : k + 1, :].astype(F32) * items[...].astype(F32)
        ).astype(BF16)
    tensor_res[...] = (
        dot(model_di[...], user[...], 1, 1) - slab[...].reshape(128, 512).astype(F32)
    ).astype(BF16)
    projected = dot(tensor_res[...], user[...])
    item_term = jnp.zeros((32, RANK), F32)
    small[...] = jnp.zeros_like(small)
    for k in range(4):
        part = projected[32 * k : 32 * k + 32, :]
        item_term = item_term + part * domains[k : k + 1, :].astype(F32)
        small[32 + k : 33 + k, :] = DOMAIN_SCALE * jnp.sum(
            part * items[...].astype(F32), axis=0, keepdims=True
        )
    small[0:32, :] = ITEM_SCALE * item_term
    small_abs[...] = small[...].T.reshape(32, ROWS, 128)
    for slot in range(NZ):
        sx_other[slot] = small_abs[absolute(1, slot)].astype(BF16)
        sx_own[slot] = small_abs[absolute(0, slot)]
    sx_state = reduce_start(sx_other, sx_x)

    ut_abs[...] = user[...].T.reshape(32, ROWS, 512)
    for plane in range(2):
        for slot in range(NZ):
            ut_rel[plane, slot] = ut_abs[absolute(plane, slot)]
    user_rel[...] = ut_rel[...].reshape(512, 512).T
    tensor_user[...] = (
        TENSOR_SCALE * dot(model_di[...], tensor_res[...], 0, 0)
    ).reshape(32, ROWS, 512)

    for c in range(CHUNKS):
        gather_own(panel.at[c], gathers[c])
    for i in range(3):
        reduce_near(sx_own, sx_x, sx_send, sx_near, sx_state, i)
    for c in range(CHUNKS):
        gather_hubs(panel.at[c], gathers[c], 1)
    for i in range(3):
        reduce_far(sx_own, sx_near, sx_hub, sx_far, sx_state, i)
    for c in range(CHUNKS):
        gather_near(panel.at[c], gathers[c], 1)
    for c in range(CHUNKS):
        gather_hubs(panel.at[c], gathers[c], 3)
    for c in range(CHUNKS):
        gather_near(panel.at[c], gathers[c], 3)

    total = reduce_end(sx_own, sx_far, sx_state)
    row_send[...] = total
    row_copies = [send(row_send, row_recv.at[0], partner)]
    row_copies += [send(row_send, row_recv.at[dy], beside(dy)) for dy in range(1, 4)]

    side_copy.wait()
    gf_state = []

    def compute(c):
        gather_end(gathers[c])
        blocks = [panel[c, p].reshape(18 * ROWS, width)[0:256] for p in range(2)]
        model = dot(user_rel[:, 0:256], blocks[0]) + dot(user_rel[:, 256:512], blocks[1])
        res = (model - side[:, c * width : (c + 1) * width].astype(F32)).astype(BF16)
        gf_other[c] = dot(ut_rel[1].reshape(256, 512), res).reshape(NZ, ROWS, width).astype(BF16)
        gf_state.append(reduce_start(gf_other.at[c], gf_x.at[c]))
        gf_own[c] = dot(ut_rel[0].reshape(256, 512), res).reshape(NZ, ROWS, width)
        for p in range(2):
            part = dot(blocks[p], res, 1, 1).reshape(NZ, ROWS, 512)
            side_user[p] = part if c == 0 else side_user[p] + part

    compute(0)
    compute(1)

    for copy in row_copies:
        copy.wait_recv()
    lane = lax.broadcasted_iota(jnp.int32, (ROWS, 128), 1)
    row_y[...] = row_send[...] + row_recv[1] + row_recv[2] + row_recv[3]
    row_copy = send(row_y, row_recv.at[4], opposite)

    for plane in range(2):
        for slot in range(NZ):
            b = absolute(plane, slot)
            place = (b // 2 + d) % 2 * 16 + b // 4 * 2 + b % 2
            su_all[place] = SIDE_SCALE * side_user[plane, slot] + tensor_user[b]
    su_core[...] = su_all[16:].astype(BF16)
    su_copy = send(su_core, su_core_recv, partner)

    def gf_near_step(c, i):
        reduce_near(gf_own.at[c], gf_x.at[c], gf_send.at[c], gf_near.at[c], gf_state[c], i)

    def gf_far_step(c, i):
        reduce_far(gf_own.at[c], gf_near.at[c], gf_hub.at[c], gf_far.at[c], gf_state[c], i)

    gf_near_step(0, 0)
    su_copy.wait_recv()
    su_sum[...] = (su_all[:16] + su_core_recv[...].astype(F32)).reshape(8, 32, 512)
    su_send[...] = su_sum[...].astype(BF16)
    su_copies = [
        send(su_send.at[pl.ds((y + dy) % 4 * 2, 2)], su_recv.at[dy - 1], beside(dy))
        for dy in range(1, 4)
    ]
    gf_near_step(0, 1)
    row_copy.wait_recv()
    small_panel[0, 0, 0] = jnp.where(
        lane < 32, row_send[...] + row_recv[0], row_y[...] + row_recv[4]
    )
    small_gather = gather_start(small_panel)
    gf_near_step(0, 2)
    gf_far_step(0, 0)
    gf_near_step(1, 0)
    gather_own(small_panel, small_gather)
    gf_far_step(0, 1)
    gf_near_step(1, 1)
    for copy in su_copies:
        copy.wait_recv()
    for i in range(2):
        grad = su_sum[y * 2 + i]
        for dy in range(3):
            grad = grad + su_recv[dy, i].astype(F32)
        su_y[i] = grad
    su_copy = send(su_y.at[1 - xh], su_x, opposite)
    gf_far_step(1, 0)
    gf_near_step(1, 2)
    gather_hubs(small_panel, small_gather, 1)
    gf_far_step(1, 1)
    gf_far_step(0, 2)
    gf_far_step(1, 2)
    gather_near(small_panel, small_gather, 1)
    gather_hubs(small_panel, small_gather, 3)
    gather_near(small_panel, small_gather, 3)

    su_copy.wait_recv()
    gu_ref[...] = su_y[xh] + su_x[...]
    gf_ref[:, 0:width] = FEAT_SCALE * reduce_end(gf_own.at[0], gf_far.at[0], gf_state[0])
    gf_ref[:, width:] = FEAT_SCALE * reduce_end(gf_own.at[1], gf_far.at[1], gf_state[1])
    gather_end(small_gather)
    for plane in range(2):
        for slot in range(NZ):
            small_abs[absolute(plane, slot)] = small_panel[plane, slot // 3, slot % 3]
    small[...] = small_abs[...].reshape(512, 128).T
    gi_ref[...] = small[0:32, :]
    gd_ref[...] = small[32:36, :]
    for copy in sent:
        copy.wait_send()


def local(side_matrix, slab, user_factor, feat_factor, item_factor, domain_factor):
    width = 1024 // CHUNKS

    def reduction(lead, w):
        return [
            pltpu.VMEM(lead + (NZ, ROWS, w), BF16),
            pltpu.VMEM(lead + (NZ, ROWS, w), F32),
            pltpu.VMEM(lead + (NZ, ROWS, w), BF16),
            pltpu.VMEM(lead + (6, 3, ROWS, w), BF16),
            pltpu.VMEM(lead + (6, 3, ROWS, w), BF16),
            pltpu.VMEM(lead + (4, ROWS, w), BF16),
            pltpu.VMEM(lead + (4, ROWS, w), BF16),
        ]

    shapes = (
        pltpu.VMEM((32, 512), F32),
        pltpu.VMEM((ROWS, 1024), F32),
        pltpu.VMEM((32, RANK), F32),
        pltpu.VMEM((4, RANK), F32),
    )
    grad_user, grad_feat, grad_item, grad_domain = pl.pallas_call(
        kernel,
        out_shape=shapes,
        in_specs=[pl.BlockSpec(memory_space=pltpu.HBM)] * 6,
        out_specs=[pl.BlockSpec(memory_space=pltpu.VMEM)] * 4,
        scratch_shapes=[
            pltpu.VMEM((512, 1024), BF16),
            pltpu.VMEM((4, 32, 512), BF16),
            pltpu.VMEM((512, 512), BF16),
            pltpu.VMEM((32, 512), BF16),
            pltpu.VMEM((4, 512), BF16),
            pltpu.VMEM((CHUNKS, 2, 6, 3, ROWS, width), BF16),
            pltpu.VMEM((512, 512), BF16),
            pltpu.VMEM((32, ROWS, 512), BF16),
            pltpu.VMEM((2, NZ, ROWS, 512), BF16),
            pltpu.VMEM((128, 512), BF16),
            pltpu.VMEM((128, 512), BF16),
            pltpu.VMEM((128, 512), F32),
            pltpu.VMEM((32, ROWS, 128), F32),
            pltpu.VMEM((32, ROWS, 512), F32),
            pltpu.VMEM((2, NZ, ROWS, 512), F32),
        ]
        + reduction((CHUNKS,), width)
        + reduction((), 128)
        + [
            pltpu.VMEM((ROWS, 128), F32),
            pltpu.VMEM((5, ROWS, 128), F32),
            pltpu.VMEM((ROWS, 128), F32),
            pltpu.VMEM((2, 6, 3, ROWS, 128), F32),
            pltpu.VMEM((32, ROWS, 512), F32),
            pltpu.VMEM((16, ROWS, 512), BF16),
            pltpu.VMEM((16, ROWS, 512), BF16),
            pltpu.VMEM((8, 32, 512), F32),
            pltpu.VMEM((8, 32, 512), BF16),
            pltpu.VMEM((3, 2, 32, 512), BF16),
            pltpu.VMEM((2, 32, 512), F32),
            pltpu.VMEM((32, 512), F32),
            pltpu.SemaphoreType.DMA((N_MESSAGES,)),
            pltpu.SemaphoreType.DMA((N_MESSAGES,)),
            pltpu.SemaphoreType.DMA((N_LOCAL,)),
        ],
        compiler_params=pltpu.CompilerParams(
            collective_id=0, has_side_effects=True, vmem_limit_bytes=63 << 20
        ),
        name="factor_gradients",
    )(side_matrix, slab, user_factor, feat_factor, item_factor, domain_factor)
    return grad_user.T, grad_feat, grad_item, grad_domain


def solution(mesh):
    return jax.shard_map(
        local,
        mesh=mesh,
        in_specs=(
            P("user", ("feat", "dom")),
            P("dom", "feat", "user"),
            P("user", None),
            P("user", ("feat", "dom")),
            P("feat", None),
            P("dom", None),
        ),
        out_specs=(
            P("user", ("feat", "dom")),
            P("user", ("feat", "dom")),
            P("feat", None),
            P("dom", None),
        ),
        check_vma=False,
    )
```

```python
import math

import jax
import jax.numpy as jnp
from jax import lax
from jax.experimental import pallas as pl
from jax.experimental.pallas import tpu as pltpu
from jax.sharding import PartitionSpec as P

MESH = pl.DeviceIdType.MESH
F32, BF16 = jnp.float32, jnp.bfloat16

RANK = 512
FEATS = 16384
ITEMS = 256
DOMS = 8
USERS = 16384

NZ = 16
ROWS = 16
CHUNKS = 2
HUBS = (0, 3, -3, 6, -6)
SLOTS = tuple(h + j for h in HUBS for j in (0, -1, 1)) + (8,)

SIDE_SCALE = math.sqrt(RANK / FEATS)
TENSOR_SCALE = math.sqrt(RANK / (ITEMS * DOMS))
FEAT_SCALE = 1.0 / math.sqrt(USERS)
ITEM_SCALE = math.sqrt(RANK / (USERS * DOMS))
DOMAIN_SCALE = 1.0 / math.sqrt(USERS * ITEMS)

N_MESSAGES = 128
N_LOCAL = 8


def dot(a, b, ca=1, cb=0):
    return lax.dot_general(a, b, (((ca,), (cb,)), ((), ())), preferred_element_type=F32)


def kernel(
    side_h, slab_h, user_h, feat_h, item_h, domain_h,
    gu_ref, gf_ref, gi_ref, gd_ref,
    side, slab, user, items, domains,
    panel, user_rel, ut_abs, ut_rel,
    model_di, tensor_res, small, small_abs, tensor_user, side_user,
    gf_own, gf_stage, gf_near, gf_other, gf_x, gf_hub, gf_far,
    sx_own, sx_stage, sx_near, sx_other, sx_x, sx_hub, sx_far,
    row_send, row_recv, row_y, small_panel,
    su_all, su_core, su_core_recv, su_sum, su_send, su_recv, su_y, su_x,
    send_sems, recv_sems, local_sems,
):
    u, f, d = lax.axis_index("user"), lax.axis_index("feat"), lax.axis_index("dom")
    xl, z, y, xh = u // NZ, u % NZ, f // 2, f % 2
    width = panel.shape[-1]

    def along(dz=0, dx=0):
        return ((xl + dx) % 2 * NZ + (z + dz + NZ) % NZ, f, d)

    def beside(dy):
        return (u, (y + dy) % 4 * 2 + xh, d)

    partner, opposite = (u, f, 1 - d), (u, y * 2 + 1 - xh, d)
    counter = [0]

    def send(src, dst, device):
        i = counter[0]
        counter[0] += 1
        copy = pltpu.make_async_remote_copy(
            src, dst, send_sems.at[i], recv_sems.at[i], device_id=device, device_id_type=MESH
        )
        copy.start()
        sent.append(copy)
        return copy

    sent = []

    feat_copies = [
        pltpu.make_async_copy(
            feat_h.at[:, pl.ds(c * width, width)], panel.at[c, 0, 0, 0], local_sems.at[c]
        )
        for c in range(CHUNKS)
    ]
    user_copy = pltpu.make_async_copy(user_h, user, local_sems.at[CHUNKS])
    item_copy = pltpu.make_async_copy(item_h, items, local_sems.at[CHUNKS + 1])
    domain_copy = pltpu.make_async_copy(domain_h, domains, local_sems.at[CHUNKS + 2])
    slab_copy = pltpu.make_async_copy(slab_h, slab, local_sems.at[CHUNKS + 3])
    side_copy = pltpu.make_async_copy(side_h, side, local_sems.at[CHUNKS + 4])
    for copy in feat_copies + [user_copy, item_copy, domain_copy, slab_copy, side_copy]:
        copy.start()

    barrier = pltpu.get_barrier_semaphore()
    greet = [along(dz) for dz in (1, -1, 2, -2, 3, -3)] + [along(0, 1), partner]
    greet += [beside(dy) for dy in range(1, 4)] + [opposite]
    for device in greet:
        pl.semaphore_signal(barrier, inc=1, device_id=device, device_id_type=MESH)
    pl.semaphore_wait(barrier, len(greet))

    def to_neighbours(g, state, plane, groups):
        hub = g.at[plane, groups, 0]
        state["near"].append(send(hub, g.at[plane, groups, 1], along(1)))
        state["near"].append(send(hub, g.at[plane, groups, 2], along(-1)))

    def to_far_end(g, state, plane):
        state["near"].append(send(g.at[plane, 3, 0], g.at[plane, 5, 0], along(-2)))

    def gather_start(g):
        own = g.at[0, 0, 0]
        far = [send(own, g.at[0, h, 0], along(-HUBS[h])) for h in (1, 2)]
        other = send(own, g.at[1, 0, 0], along(0, 1))
        state = {"far": far, "other": other, "near": []}
        to_neighbours(g, state, 0, 0)
        return state

    def gather_own(g, state):
        state["other"].wait_recv()
        to_neighbours(g, state, 1, 0)

    def gather_hubs(g, state, lo):
        for copy in state["far"]:
            copy.wait_recv()
        if lo == 1:
            state["far"] = [
                send(g.at[0, h, 0], g.at[0, h + 2, 0], along(-HUBS[h])) for h in (1, 2)
            ]
        two = pl.ds(lo, 2)
        state["other"] = send(g.at[0, two, 0], g.at[1, two, 0], along(0, 1))
        to_neighbours(g, state, 0, two)
        if lo == 3:
            to_far_end(g, state, 0)

    def gather_other(g, state, lo):
        state["other"].wait_recv()
        to_neighbours(g, state, 1, pl.ds(lo, 2))
        if lo == 3:
            to_far_end(g, state, 1)

    def gather_end(state):
        for copy in state["near"]:
            copy.wait_recv()

    groups = ((3, 2), (1, 2), (0, 1))

    def reduce_split(slot_value, own, stage):
        for plane in range(2):
            for slot in range(NZ):
                value, h, j = slot_value(plane, slot), slot // 3, slot % 3
                if j == 0 and h < 5:
                    own[plane, h] = value
                else:
                    stage[plane, h, j] = value.astype(BF16)

    def reduce_start(stage, near):
        state = {"near": [], "other": [], "far": []}
        for first, count in groups:
            some = pl.ds(first, count)
            copies = [
                send(stage.at[:, some, 2], near.at[:, some, 2], along(1)),
                send(stage.at[:, some, 1], near.at[:, some, 1], along(-1)),
            ]
            if first == 3:
                copies.append(send(stage.at[:, 5, 0], near.at[:, 5, 0], along(2)))
            state["near"].append(copies)
        return state

    def reduce_hubs(own, near, other, x, state, i):
        for copy in state["near"][i]:
            copy.wait_recv()
        first, count = groups[i]
        for h in range(first, first + count):
            total = own[:, h] + near[:, h, 1].astype(F32) + near[:, h, 2].astype(F32)
            if h == 3:
                total = total + near[:, 5, 0].astype(F32)
            own[0, h] = total[0]
            other[h] = total[1].astype(BF16)
        some = pl.ds(first, count)
        state["other"].append(send(other.at[some], x.at[some], along(0, 1)))

    def reduce_far(own, x, hub, far, state, i):
        state["other"][i].wait_recv()
        first, count = groups[i]
        for h in range(first, first + count):
            total = own[0, h] + x[h].astype(F32)
            if h == 0:
                own[0, 0] = total
            else:
                hub[h - 1] = total.astype(BF16)
                state["far"].append(send(hub.at[h - 1], far.at[h - 1], along(HUBS[h])))

    def reduce_end(own, far, state):
        for copy in state["far"]:
            copy.wait_recv()
        total = own[0, 0]
        for h in range(4):
            total = total + far[h].astype(F32)
        return total

    gathers = []
    for c in range(CHUNKS):
        feat_copies[c].wait()
        gathers.append(gather_start(panel.at[c]))

    def absolute(plane, slot):
        return (xl + plane) % 2 * NZ + (z + SLOTS[slot] + NZ) % NZ

    user_copy.wait()
    item_copy.wait()
    domain_copy.wait()
    slab_copy.wait()
    for k in range(4):
        model_di[32 * k : 32 * k + 32, :] = (
            domains[k : k + 1, :].astype(F32) * items[...].astype(F32)
        ).astype(BF16)
    tensor_res[...] = (
        dot(model_di[...], user[...], 1, 1) - slab[...].reshape(128, 512).astype(F32)
    ).astype(BF16)
    projected = dot(tensor_res[...], user[...])
    item_term = jnp.zeros((32, RANK), F32)
    small[...] = jnp.zeros_like(small)
    for k in range(4):
        part = projected[32 * k : 32 * k + 32, :]
        item_term = item_term + part * domains[k : k + 1, :].astype(F32)
        small[32 + k : 33 + k, :] = DOMAIN_SCALE * jnp.sum(
            part * items[...].astype(F32), axis=0, keepdims=True
        )
    small[0:32, :] = ITEM_SCALE * item_term
    small_abs[...] = small[...].T.reshape(32, ROWS, 128)
    reduce_split(lambda plane, slot: small_abs[absolute(plane, slot)], sx_own, sx_stage)
    sx_state = reduce_start(sx_stage, sx_near)

    ut_abs[...] = user[...].T.reshape(32, ROWS, 512)
    for plane in range(2):
        for slot in range(NZ):
            ut_rel[plane, slot] = ut_abs[absolute(plane, slot)]
    user_rel[...] = ut_rel[...].reshape(512, 512).T
    tensor_user[...] = (
        TENSOR_SCALE * dot(model_di[...], tensor_res[...], 0, 0)
    ).reshape(32, ROWS, 512)

    def each(step, *more):
        for c in range(CHUNKS):
            step(panel.at[c], gathers[c], *more)

    each(gather_own)
    for i in range(3):
        reduce_hubs(sx_own, sx_near, sx_other, sx_x, sx_state, i)
    each(gather_hubs, 1)
    for i in range(3):
        reduce_far(sx_own, sx_x, sx_hub, sx_far, sx_state, i)
    each(gather_other, 1)
    each(gather_hubs, 3)
    each(gather_other, 3)

    row_send[...] = reduce_end(sx_own, sx_far, sx_state)
    row_copies = [send(row_send, row_recv.at[0], partner)]
    row_copies += [send(row_send, row_recv.at[dy], beside(dy)) for dy in range(1, 4)]

    side_copy.wait()
    gf_state = []

    def compute(c):
        gather_end(gathers[c])
        blocks = [panel[c, p].reshape(18 * ROWS, width)[0:256] for p in range(2)]
        model = dot(user_rel[:, 0:256], blocks[0]) + dot(user_rel[:, 256:512], blocks[1])
        res = (model - side[:, c * width : (c + 1) * width].astype(F32)).astype(BF16)
        part = dot(ut_rel[...].reshape(512, 512), res).reshape(2, NZ, ROWS, width)
        reduce_split(lambda plane, slot: part[plane, slot], gf_own.at[c], gf_stage.at[c])
        gf_state.append(reduce_start(gf_stage.at[c], gf_near.at[c]))
        for p in range(2):
            user_part = dot(blocks[p], res, 1, 1).reshape(NZ, ROWS, 512)
            side_user[p] = user_part if c == 0 else side_user[p] + user_part

    compute(0)
    for copy in row_copies:
        copy.wait_recv()
    lane = lax.broadcasted_iota(jnp.int32, (ROWS, 128), 1)
    row_y[...] = row_send[...] + row_recv[1] + row_recv[2] + row_recv[3]
    row_copy = send(row_y, row_recv.at[4], opposite)
    compute(1)

    for plane in range(2):
        for slot in range(NZ):
            b = absolute(plane, slot)
            place = (b // 2 + d) % 2 * 16 + b // 4 * 2 + b % 2
            su_all[place] = SIDE_SCALE * side_user[plane, slot] + tensor_user[b]
    su_core[...] = su_all[16:].astype(BF16)
    su_copy = send(su_core, su_core_recv, partner)

    def hubs_step(c, i):
        reduce_hubs(gf_own.at[c], gf_near.at[c], gf_other.at[c], gf_x.at[c], gf_state[c], i)

    def far_step(c, i):
        reduce_far(gf_own.at[c], gf_x.at[c], gf_hub.at[c], gf_far.at[c], gf_state[c], i)

    hubs_step(0, 0)
    row_copy.wait_recv()
    small_panel[0, 0, 0] = jnp.where(
        lane < 32, row_send[...] + row_recv[0], row_y[...] + row_recv[4]
    )
    small_gather = gather_start(small_panel)
    hubs_step(0, 1)
    hubs_step(0, 2)
    hubs_step(1, 0)
    su_copy.wait_recv()
    su_sum[...] = (su_all[:16] + su_core_recv[...].astype(F32)).reshape(8, 32, 512)
    su_send[...] = su_sum[...].astype(BF16)
    su_copies = [
        send(su_send.at[pl.ds((y + dy) % 4 * 2, 2)], su_recv.at[dy - 1], beside(dy))
        for dy in range(1, 4)
    ]
    hubs_step(1, 1)
    hubs_step(1, 2)
    far_step(0, 0)
    gather_own(small_panel, small_gather)
    far_step(0, 1)
    far_step(0, 2)
    far_step(1, 0)
    gather_hubs(small_panel, small_gather, 1)
    far_step(1, 1)
    far_step(1, 2)
    for copy in su_copies:
        copy.wait_recv()
    for i in range(2):
        grad = su_sum[y * 2 + i]
        for dy in range(3):
            grad = grad + su_recv[dy, i].astype(F32)
        su_y[i] = grad
    su_copy = send(su_y.at[1 - xh], su_x, opposite)
    gather_other(small_panel, small_gather, 1)
    gather_hubs(small_panel, small_gather, 3)
    su_copy.wait_recv()
    gu_ref[...] = su_y[xh] + su_x[...]
    gather_other(small_panel, small_gather, 3)
    for c in range(CHUNKS):
        gf_ref[:, c * width : (c + 1) * width] = FEAT_SCALE * reduce_end(
            gf_own.at[c], gf_far.at[c], gf_state[c]
        )
    gather_end(small_gather)
    for plane in range(2):
        for slot in range(NZ):
            small_abs[absolute(plane, slot)] = small_panel[plane, slot // 3, slot % 3]
    small[...] = small_abs[...].reshape(512, 128).T
    gi_ref[...] = small[0:32, :]
    gd_ref[...] = small[32:36, :]
    for copy in sent:
        copy.wait_send()


def local(side_matrix, slab, user_factor, feat_factor, item_factor, domain_factor):
    width = 1024 // CHUNKS

    def reduction(lead, w):
        return [
            pltpu.VMEM(lead + (2, 5, ROWS, w), F32),
            pltpu.VMEM(lead + (2, 6, 3, ROWS, w), BF16),
            pltpu.VMEM(lead + (2, 6, 3, ROWS, w), BF16),
            pltpu.VMEM(lead + (5, ROWS, w), BF16),
            pltpu.VMEM(lead + (5, ROWS, w), BF16),
            pltpu.VMEM(lead + (4, ROWS, w), BF16),
            pltpu.VMEM(lead + (4, ROWS, w), BF16),
        ]

    shapes = (
        pltpu.VMEM((32, 512), F32),
        pltpu.VMEM((ROWS, 1024), F32),
        pltpu.VMEM((32, RANK), F32),
        pltpu.VMEM((4, RANK), F32),
    )
    grad_user, grad_feat, grad_item, grad_domain = pl.pallas_call(
        kernel,
        out_shape=shapes,
        in_specs=[pl.BlockSpec(memory_space=pltpu.HBM)] * 6,
        out_specs=[pl.BlockSpec(memory_space=pltpu.VMEM)] * 4,
        scratch_shapes=[
            pltpu.VMEM((512, 1024), BF16),
            pltpu.VMEM((4, 32, 512), BF16),
            pltpu.VMEM((512, 512), BF16),
            pltpu.VMEM((32, 512), BF16),
            pltpu.VMEM((4, 512), BF16),
            pltpu.VMEM((CHUNKS, 2, 6, 3, ROWS, width), BF16),
            pltpu.VMEM((512, 512), BF16),
            pltpu.VMEM((32, ROWS, 512), BF16),
            pltpu.VMEM((2, NZ, ROWS, 512), BF16),
            pltpu.VMEM((128, 512), BF16),
            pltpu.VMEM((128, 512), BF16),
            pltpu.VMEM((128, 512), F32),
            pltpu.VMEM((32, ROWS, 128), F32),
            pltpu.VMEM((32, ROWS, 512), F32),
            pltpu.VMEM((2, NZ, ROWS, 512), F32),
        ]
        + reduction((CHUNKS,), width)
        + reduction((), 128)
        + [
            pltpu.VMEM((ROWS, 128), F32),
            pltpu.VMEM((5, ROWS, 128), F32),
            pltpu.VMEM((ROWS, 128), F32),
            pltpu.VMEM((2, 6, 3, ROWS, 128), F32),
            pltpu.VMEM((32, ROWS, 512), F32),
            pltpu.VMEM((16, ROWS, 512), BF16),
            pltpu.VMEM((16, ROWS, 512), BF16),
            pltpu.VMEM((8, 32, 512), F32),
            pltpu.VMEM((8, 32, 512), BF16),
            pltpu.VMEM((3, 2, 32, 512), BF16),
            pltpu.VMEM((2, 32, 512), F32),
            pltpu.VMEM((32, 512), F32),
            pltpu.SemaphoreType.DMA((N_MESSAGES,)),
            pltpu.SemaphoreType.DMA((N_MESSAGES,)),
            pltpu.SemaphoreType.DMA((N_LOCAL,)),
        ],
        compiler_params=pltpu.CompilerParams(
            collective_id=0, has_side_effects=True, vmem_limit_bytes=63 << 20
        ),
        name="factor_gradients",
    )(side_matrix, slab, user_factor, feat_factor, item_factor, domain_factor)
    return grad_user.T, grad_feat, grad_item, grad_domain


def solution(mesh):
    return jax.shard_map(
        local,
        mesh=mesh,
        in_specs=(
            P("user", ("feat", "dom")),
            P("dom", "feat", "user"),
            P("user", None),
            P("user", ("feat", "dom")),
            P("feat", None),
            P("dom", None),
        ),
        out_specs=(
            P("user", ("feat", "dom")),
            P("user", ("feat", "dom")),
            P("feat", None),
            P("dom", None),
        ),
        check_vma=False,
    )
```

```python
import math

import jax
import jax.numpy as jnp
from jax import lax
from jax.experimental import pallas as pl
from jax.experimental.pallas import tpu as pltpu
from jax.sharding import PartitionSpec as P

MESH = pl.DeviceIdType.MESH
F32, BF16 = jnp.float32, jnp.bfloat16

RANK = 512
FEATS = 16384
ITEMS = 256
DOMS = 8
USERS = 16384

NZ = 16
ROWS = 16
CHUNKS = 2
HUBS = (0, 3, -3, 6, -6)
SLOTS = tuple(h + j for h in HUBS for j in (0, -1, 1)) + (8,)

SIDE_SCALE = math.sqrt(RANK / FEATS)
TENSOR_SCALE = math.sqrt(RANK / (ITEMS * DOMS))
FEAT_SCALE = 1.0 / math.sqrt(USERS)
ITEM_SCALE = math.sqrt(RANK / (USERS * DOMS))
DOMAIN_SCALE = 1.0 / math.sqrt(USERS * ITEMS)

N_MESSAGES = 128
N_LOCAL = 8


def dot(a, b, ca=1, cb=0):
    return lax.dot_general(a, b, (((ca,), (cb,)), ((), ())), preferred_element_type=F32)


def kernel(
    side_h, slab_h, user_h, feat_h, item_h, domain_h,
    gu_ref, gf_ref, gi_ref, gd_ref,
    side, slab, user, items, domains,
    panel, user_rel, ut_abs, ut_rel,
    model_di, tensor_res, small, small_abs, tensor_user, side_user,
    gf_own, gf_stage, gf_near, gf_other, gf_x, gf_hub, gf_far,
    sx_own, sx_stage, sx_near, sx_other, sx_x, sx_hub, sx_far,
    row_send, row_recv, row_y, small_panel,
    su_all, su_core, su_core_recv, su_sum, su_send, su_recv, su_y, su_x,
    send_sems, recv_sems, local_sems,
):
    u, f, d = lax.axis_index("user"), lax.axis_index("feat"), lax.axis_index("dom")
    xl, z, y, xh = u // NZ, u % NZ, f // 2, f % 2
    width = panel.shape[-1]

    def along(dz=0, dx=0):
        return ((xl + dx) % 2 * NZ + (z + dz + NZ) % NZ, f, d)

    def beside(dy):
        return (u, (y + dy) % 4 * 2 + xh, d)

    partner, opposite = (u, f, 1 - d), (u, y * 2 + 1 - xh, d)
    counter = [0]

    def send(src, dst, device):
        i = counter[0]
        counter[0] += 1
        copy = pltpu.make_async_remote_copy(
            src, dst, send_sems.at[i], recv_sems.at[i], device_id=device, device_id_type=MESH
        )
        copy.start()
        sent.append(copy)
        return copy

    sent = []

    feat_copies = [
        pltpu.make_async_copy(
            feat_h.at[:, pl.ds(c * width, width)], panel.at[c, 0, 0, 0], local_sems.at[c]
        )
        for c in range(CHUNKS)
    ]
    user_copy = pltpu.make_async_copy(user_h, user, local_sems.at[CHUNKS])
    item_copy = pltpu.make_async_copy(item_h, items, local_sems.at[CHUNKS + 1])
    domain_copy = pltpu.make_async_copy(domain_h, domains, local_sems.at[CHUNKS + 2])
    slab_copy = pltpu.make_async_copy(slab_h, slab, local_sems.at[CHUNKS + 3])
    side_copy = pltpu.make_async_copy(side_h, side, local_sems.at[CHUNKS + 4])
    for copy in feat_copies + [user_copy, item_copy, domain_copy, slab_copy, side_copy]:
        copy.start()

    barrier = pltpu.get_barrier_semaphore()
    greet = [along(dz) for dz in (1, -1, 2, -2, 3, -3)] + [along(0, 1), partner]
    greet += [beside(dy) for dy in range(1, 4)] + [opposite]
    for device in greet:
        pl.semaphore_signal(barrier, inc=1, device_id=device, device_id_type=MESH)
    pl.semaphore_wait(barrier, len(greet))

    def to_neighbours(g, state, plane, groups):
        hub = g.at[plane, groups, 0]
        state["near"].append(send(hub, g.at[plane, groups, 1], along(1)))
        state["near"].append(send(hub, g.at[plane, groups, 2], along(-1)))

    def to_far_end(g, state, plane):
        state["near"].append(send(g.at[plane, 3, 0], g.at[plane, 5, 0], along(-2)))

    def gather_start(g):
        own = g.at[0, 0, 0]
        far = [send(own, g.at[0, h, 0], along(-HUBS[h])) for h in (1, 2)]
        other = send(own, g.at[1, 0, 0], along(0, 1))
        state = {"far": far, "other": other, "near": []}
        to_neighbours(g, state, 0, 0)
        return state

    def gather_own(g, state):
        state["other"].wait_recv()
        to_neighbours(g, state, 1, 0)

    def gather_hubs(g, state, lo):
        for copy in state["far"]:
            copy.wait_recv()
        if lo == 1:
            state["far"] = [
                send(g.at[0, h, 0], g.at[0, h + 2, 0], along(-HUBS[h])) for h in (1, 2)
            ]
        two = pl.ds(lo, 2)
        state["other"] = send(g.at[0, two, 0], g.at[1, two, 0], along(0, 1))
        to_neighbours(g, state, 0, two)
        if lo == 3:
            to_far_end(g, state, 0)

    def gather_other(g, state, lo):
        state["other"].wait_recv()
        to_neighbours(g, state, 1, pl.ds(lo, 2))
        if lo == 3:
            to_far_end(g, state, 1)

    def gather_end(state):
        for copy in state["near"]:
            copy.wait_recv()

    groups = ((3, 2), (1, 2), (0, 1))

    def reduce_split(slot_value, own, stage):
        for plane in range(2):
            for slot in range(NZ):
                value, h, j = slot_value(plane, slot), slot // 3, slot % 3
                if j == 0 and h < 5:
                    own[plane, h] = value
                else:
                    stage[plane, h, j] = value.astype(BF16)

    def reduce_start(stage, near):
        state = {"near": [], "other": [], "far": []}
        for first, count in groups:
            some = pl.ds(first, count)
            copies = [
                send(stage.at[:, some, 2], near.at[:, some, 2], along(1)),
                send(stage.at[:, some, 1], near.at[:, some, 1], along(-1)),
            ]
            if first == 3:
                copies.append(send(stage.at[:, 5, 0], near.at[:, 5, 0], along(2)))
            state["near"].append(copies)
        return state

    def reduce_hubs(own, near, other, x, state, i):
        for copy in state["near"][i]:
            copy.wait_recv()
        first, count = groups[i]
        for h in range(first, first + count):
            total = own[:, h] + near[:, h, 1].astype(F32) + near[:, h, 2].astype(F32)
            if h == 3:
                total = total + near[:, 5, 0].astype(F32)
            own[0, h] = total[0]
            other[h] = total[1].astype(BF16)
        some = pl.ds(first, count)
        state["other"].append(send(other.at[some], x.at[some], along(0, 1)))

    def reduce_far(own, x, hub, far, state, i):
        state["other"][i].wait_recv()
        first, count = groups[i]
        for h in range(first, first + count):
            total = own[0, h] + x[h].astype(F32)
            if h == 0:
                own[0, 0] = total
            else:
                hub[h - 1] = total.astype(BF16)
                state["far"].append(send(hub.at[h - 1], far.at[h - 1], along(HUBS[h])))

    def reduce_end(own, far, state):
        for copy in state["far"]:
            copy.wait_recv()
        total = own[0, 0]
        for h in range(4):
            total = total + far[h].astype(F32)
        return total

    gathers = []
    for c in range(CHUNKS):
        feat_copies[c].wait()
        gathers.append(gather_start(panel.at[c]))

    def absolute(plane, slot):
        return (xl + plane) % 2 * NZ + (z + SLOTS[slot] + NZ) % NZ

    user_copy.wait()
    item_copy.wait()
    domain_copy.wait()
    slab_copy.wait()
    for k in range(4):
        model_di[32 * k : 32 * k + 32, :] = (
            domains[k : k + 1, :].astype(F32) * items[...].astype(F32)
        ).astype(BF16)
    tensor_res[...] = (
        dot(model_di[...], user[...], 1, 1) - slab[...].reshape(128, 512).astype(F32)
    ).astype(BF16)
    projected = dot(tensor_res[...], user[...])
    item_term = jnp.zeros((32, RANK), F32)
    small[...] = jnp.zeros_like(small)
    for k in range(4):
        part = projected[32 * k : 32 * k + 32, :]
        item_term = item_term + part * domains[k : k + 1, :].astype(F32)
        small[32 + k : 33 + k, :] = DOMAIN_SCALE * jnp.sum(
            part * items[...].astype(F32), axis=0, keepdims=True
        )
    small[0:32, :] = ITEM_SCALE * item_term
    small_abs[...] = small[...].T.reshape(32, ROWS, 128)
    reduce_split(lambda plane, slot: small_abs[absolute(plane, slot)], sx_own, sx_stage)
    sx_state = reduce_start(sx_stage, sx_near)

    ut_abs[...] = user[...].T.reshape(32, ROWS, 512)
    for plane in range(2):
        for slot in range(NZ):
            ut_rel[plane, slot] = ut_abs[absolute(plane, slot)]
    user_rel[...] = ut_rel[...].reshape(512, 512).T
    tensor_user[...] = (
        TENSOR_SCALE * dot(model_di[...], tensor_res[...], 0, 0)
    ).reshape(32, ROWS, 512)

    def each(step, *more):
        for c in range(CHUNKS):
            step(panel.at[c], gathers[c], *more)

    each(gather_own)
    for i in range(3):
        reduce_hubs(sx_own, sx_near, sx_other, sx_x, sx_state, i)
    each(gather_hubs, 1)
    for i in range(3):
        reduce_far(sx_own, sx_x, sx_hub, sx_far, sx_state, i)
    each(gather_other, 1)
    each(gather_hubs, 3)
    row_send[...] = reduce_end(sx_own, sx_far, sx_state)
    row_copies = [send(row_send, row_recv.at[0], partner)]
    row_copies += [send(row_send, row_recv.at[dy], beside(dy)) for dy in range(1, 4)]

    each(gather_other, 3)
    side_copy.wait()
    gf_state = []

    def compute(c):
        gather_end(gathers[c])
        blocks = [panel[c, p].reshape(18 * ROWS, width)[0:256] for p in range(2)]
        model = dot(user_rel[:, 0:256], blocks[0]) + dot(user_rel[:, 256:512], blocks[1])
        res = (model - side[:, c * width : (c + 1) * width].astype(F32)).astype(BF16)
        part = dot(ut_rel[...].reshape(512, 512), res).reshape(2, NZ, ROWS, width)
        reduce_split(lambda plane, slot: part[plane, slot], gf_own.at[c], gf_stage.at[c])
        gf_state.append(reduce_start(gf_stage.at[c], gf_near.at[c]))
        for p in range(2):
            user_part = dot(blocks[p], res, 1, 1).reshape(NZ, ROWS, 512)
            side_user[p] = user_part if c == 0 else side_user[p] + user_part

    for copy in row_copies:
        copy.wait_recv()
    lane = lax.broadcasted_iota(jnp.int32, (ROWS, 128), 1)
    row_y[...] = row_send[...] + row_recv[1] + row_recv[2] + row_recv[3]
    row_copy = send(row_y, row_recv.at[4], opposite)

    compute(0)
    compute(1)

    row_copy.wait_recv()
    mine = jnp.where(lane < 32, row_send[...] + row_recv[0], row_y[...] + row_recv[4])
    small_panel[0, 0] = jnp.concatenate([mine[0:8, 0:64], mine[8:16, 0:64]], axis=1)
    small_copies = [
        send(small_panel.at[0, 0], small_panel.at[plane, slot], along(-SLOTS[slot], plane))
        for slot in range(NZ - 1, -1, -1)
        for plane in range(2)
        if slot + plane > 0
    ]

    for plane in range(2):
        for slot in range(NZ):
            b = absolute(plane, slot)
            place = (b // 2 + d) % 2 * 16 + b // 4 * 2 + b % 2
            su_all[place] = SIDE_SCALE * side_user[plane, slot] + tensor_user[b]
    su_core[...] = su_all[16:].astype(BF16)
    su_copy = send(su_core, su_core_recv, partner)

    def hubs_step(c, i):
        reduce_hubs(gf_own.at[c], gf_near.at[c], gf_other.at[c], gf_x.at[c], gf_state[c], i)

    def far_step(c, i):
        reduce_far(gf_own.at[c], gf_x.at[c], gf_hub.at[c], gf_far.at[c], gf_state[c], i)

    for i in range(3):
        hubs_step(0, i)
    hubs_step(1, 0)
    su_copy.wait_recv()
    su_sum[...] = (su_all[:16] + su_core_recv[...].astype(F32)).reshape(8, 32, 512)
    su_send[...] = su_sum[...].astype(BF16)
    su_copies = [
        send(su_send.at[pl.ds((y + dy) % 4 * 2, 2)], su_recv.at[dy - 1], beside(dy))
        for dy in range(1, 4)
    ]
    hubs_step(1, 1)
    hubs_step(1, 2)
    for i in range(3):
        far_step(0, i)
    far_step(1, 0)
    far_step(1, 1)
    far_step(1, 2)
    for copy in su_copies:
        copy.wait_recv()
    for i in range(2):
        grad = su_sum[y * 2 + i]
        for dy in range(3):
            grad = grad + su_recv[dy, i].astype(F32)
        su_y[i] = grad
    su_copy = send(su_y.at[1 - xh], su_x, opposite)
    su_copy.wait_recv()
    gu_ref[...] = su_y[xh] + su_x[...]
    for c in range(CHUNKS):
        gf_ref[:, c * width : (c + 1) * width] = FEAT_SCALE * reduce_end(
            gf_own.at[c], gf_far.at[c], gf_state[c]
        )
    for copy in small_copies:
        copy.wait_recv()
    for plane in range(2):
        for slot in range(NZ):
            b, both = absolute(plane, slot), small_panel[plane, slot]
            small_abs[b, 0:8] = both
            small_abs[b, 8:16] = jnp.concatenate([both[:, 64:], both[:, :64]], axis=1)
    small[...] = small_abs[...].reshape(512, 128).T
    gi_ref[...] = small[0:32, :]
    gd_ref[...] = small[32:36, :]
    for copy in sent:
        copy.wait_send()


def local(side_matrix, slab, user_factor, feat_factor, item_factor, domain_factor):
    width = 1024 // CHUNKS

    def reduction(lead, w):
        return [
            pltpu.VMEM(lead + (2, 5, ROWS, w), F32),
            pltpu.VMEM(lead + (2, 6, 3, ROWS, w), BF16),
            pltpu.VMEM(lead + (2, 6, 3, ROWS, w), BF16),
            pltpu.VMEM(lead + (5, ROWS, w), BF16),
            pltpu.VMEM(lead + (5, ROWS, w), BF16),
            pltpu.VMEM(lead + (4, ROWS, w), BF16),
            pltpu.VMEM(lead + (4, ROWS, w), BF16),
        ]

    shapes = (
        pltpu.VMEM((32, 512), F32),
        pltpu.VMEM((ROWS, 1024), F32),
        pltpu.VMEM((32, RANK), F32),
        pltpu.VMEM((4, RANK), F32),
    )
    grad_user, grad_feat, grad_item, grad_domain = pl.pallas_call(
        kernel,
        out_shape=shapes,
        in_specs=[pl.BlockSpec(memory_space=pltpu.HBM)] * 6,
        out_specs=[pl.BlockSpec(memory_space=pltpu.VMEM)] * 4,
        scratch_shapes=[
            pltpu.VMEM((512, 1024), BF16),
            pltpu.VMEM((4, 32, 512), BF16),
            pltpu.VMEM((512, 512), BF16),
            pltpu.VMEM((32, 512), BF16),
            pltpu.VMEM((4, 512), BF16),
            pltpu.VMEM((CHUNKS, 2, 6, 3, ROWS, width), BF16),
            pltpu.VMEM((512, 512), BF16),
            pltpu.VMEM((32, ROWS, 512), BF16),
            pltpu.VMEM((2, NZ, ROWS, 512), BF16),
            pltpu.VMEM((128, 512), BF16),
            pltpu.VMEM((128, 512), BF16),
            pltpu.VMEM((128, 512), F32),
            pltpu.VMEM((32, ROWS, 128), F32),
            pltpu.VMEM((32, ROWS, 512), F32),
            pltpu.VMEM((2, NZ, ROWS, 512), F32),
        ]
        + reduction((CHUNKS,), width)
        + reduction((), 128)
        + [
            pltpu.VMEM((ROWS, 128), F32),
            pltpu.VMEM((5, ROWS, 128), F32),
            pltpu.VMEM((ROWS, 128), F32),
            pltpu.VMEM((2, NZ, 8, 128), F32),
            pltpu.VMEM((32, ROWS, 512), F32),
            pltpu.VMEM((16, ROWS, 512), BF16),
            pltpu.VMEM((16, ROWS, 512), BF16),
            pltpu.VMEM((8, 32, 512), F32),
            pltpu.VMEM((8, 32, 512), BF16),
            pltpu.VMEM((3, 2, 32, 512), BF16),
            pltpu.VMEM((2, 32, 512), F32),
            pltpu.VMEM((32, 512), F32),
            pltpu.SemaphoreType.DMA((N_MESSAGES,)),
            pltpu.SemaphoreType.DMA((N_MESSAGES,)),
            pltpu.SemaphoreType.DMA((N_LOCAL,)),
        ],
        compiler_params=pltpu.CompilerParams(
            collective_id=0, has_side_effects=True, vmem_limit_bytes=63 << 20
        ),
        name="factor_gradients",
    )(side_matrix, slab, user_factor, feat_factor, item_factor, domain_factor)
    return grad_user.T, grad_feat, grad_item, grad_domain


def solution(mesh):
    return jax.shard_map(
        local,
        mesh=mesh,
        in_specs=(
            P("user", ("feat", "dom")),
            P("dom", "feat", "user"),
            P("user", None),
            P("user", ("feat", "dom")),
            P("feat", None),
            P("dom", None),
        ),
        out_specs=(
            P("user", ("feat", "dom")),
            P("user", ("feat", "dom")),
            P("feat", None),
            P("dom", None),
        ),
        check_vma=False,
    )
```
